1024 devices in a mesh: expert: 32 (over z_lo, x), fsdp: 32 (over z_hi, y, core).
Axes of the slice: x: 4, y: 4, z: 32 (z_hi: 4, z_lo: 8; z = z_hi * 8 + z_lo), core: 2. Of those that a mesh axis runs over, the one named last changes fastest.
Arguments:
- tokens: bfloat16 [4096, 4096], P('fsdp', 'expert'), may hold values from -6 to 6
- out_grad: bfloat16 [4096, 4096], P('fsdp', 'expert'), may hold values from -6 to 6
- route_probs: float32 [4096, 8], P('fsdp'), may hold values from 0.1 to 1
- expert_ids: int32 [4096, 8], P('fsdp'), may hold values from 0 to 127, as said below
- gate_weight: bfloat16 [4096, 6144], P('fsdp', 'expert'), may hold values from -0.09375 to 0.09375
- up_weight: bfloat16 [4096, 6144], P('fsdp', 'expert'), may hold values from -0.09375 to 0.09375
- down_weight: bfloat16 [6144, 4096], P('expert', 'fsdp'), may hold values from -0.15625 to 0.15625
Outputs:
- x_grad: bfloat16 [4096, 4096], P('fsdp', 'expert')
- gate_grad: bfloat16 [4096, 6144], P('fsdp', 'expert')
- up_grad: bfloat16 [4096, 6144], P('fsdp', 'expert')
- down_grad: bfloat16 [6144, 4096], P('expert', 'fsdp')
The draws below stay inside these ranges and needn't reach their ends.
Inputs may be any that keep to these rules, and one draw needn't show every extreme that they name: `expert_ids`: each row names 8 different experts. In each aligned block of 128 rows every expert below 4 is named by 1 to 64 rows, and in every block one of them by exactly 64 rows.
All inputs are finite; a program needn't handle non-finite values.
Results may differ from the reference program's by a relative error of at most 0.023.
Values may be sent and summed in bfloat16 or wider, within the bound.
No kernel may reach another device: no remote copies, remote signals or barrier semaphores. Data moves between devices by JAX's collectives and lax.ppermute only.
A program may use at most 32 MiB of HBM per device.

```python
import jax
import jax.numpy as jnp
from jax import lax

D = 4096
FF = 1536
NEXP = 128
TOPK = 8
TOK_DEV = 128
CAP = 64
SLICES = 8
HID_DEV = 192
EXP_WIN = 4
TOKENS = 4096
N_EXPERT = 32
N_FSDP = 32


def draw_expert_ids(key, part):
    key = jax.random.fold_in(key, 11)
    key_count, key_pick, key_rank, key_other, key_turn = jax.random.split(key, 5)
    blocks = TOKENS // TOK_DEV
    counts = jax.random.randint(key_count, (blocks, EXP_WIN), 1, CAP + 1)
    favored = jax.random.randint(key_pick, (blocks,), 0, EXP_WIN)
    window_ids = jnp.arange(EXP_WIN, dtype=jnp.int32)
    counts = jnp.where(window_ids[None, :] == favored[:, None], CAP, counts)
    rank_scores = jax.random.randint(key_rank, (blocks, EXP_WIN, TOK_DEV), 0, 1 << 20) * TOK_DEV + jnp.arange(TOK_DEV, dtype=jnp.int32)
    ranks = jnp.argsort(jnp.argsort(rank_scores, axis=-1, stable=True), axis=-1, stable=True)
    inside = ranks < counts[:, :, None]
    inside = inside.transpose(0, 2, 1).reshape(TOKENS, EXP_WIN)
    other_scores = jax.random.randint(key_other, (TOKENS, NEXP - EXP_WIN), 0, 1 << 20) * NEXP + jnp.arange(NEXP - EXP_WIN, dtype=jnp.int32)
    others = jnp.argsort(other_scores, axis=-1, stable=True)[:, :TOPK].astype(jnp.int32) + EXP_WIN
    inside_int = inside.astype(jnp.int32)
    count_in = jnp.sum(inside_int, axis=1)
    order_in = jnp.cumsum(inside_int, axis=1) - 1
    slot_ids = jnp.arange(TOPK, dtype=jnp.int32)
    matches = inside[:, None, :] & (order_in[:, None, :] == slot_ids[None, :, None])
    window_pick = jnp.sum(jnp.where(matches, window_ids[None, None, :], 0), axis=2)
    other_index = jnp.clip(slot_ids[None, :] - count_in[:, None], 0, TOPK - 1)
    other_pick = jnp.take_along_axis(others, other_index, axis=1)
    ordered = jnp.where(slot_ids[None, :] < count_in[:, None], window_pick, other_pick)
    turn = jax.random.randint(key_turn, (TOKENS, 1), 0, TOPK)
    rotated = (slot_ids[None, :] + turn) % TOPK
    return jnp.take_along_axis(ordered, rotated, axis=1).astype(jnp.int32)


def levels(key, extent, cuts, least, top_value):
    level, own = 1.0, jax.random.fold_in(key, 6)
    for position, blocks in cuts:
        steps = jnp.exp(jax.random.uniform(jax.random.fold_in(own, position), (blocks,), jnp.float32, least / len(cuts), top_value / len(cuts)))
        level = level * jnp.repeat(steps, extent[position] // blocks).reshape([-1 if axis == position else 1 for axis in range(len(extent))])
    return level


def centred(key, shape, deviation, limit, pieces=(), held_as=jnp.bfloat16):
    result = deviation * jax.random.normal(key, shape, jnp.float32)
    if pieces:
        result = result * levels(key, shape, pieces, -0.22, 0.18)
    return jnp.clip(result, -limit, limit).astype(held_as)


def setup_inputs(seed: int = 0) -> dict:
    keys = jax.random.split(jax.random.key(seed), 8)
    tokens = centred(keys[0], (TOKENS, D), 1.0, 6.0, ((0, 32), (1, 32)))
    out_grad = centred(keys[1], (TOKENS, D), 1.0, 6.0, ((0, 32), (1, 32)))
    route_probs = jnp.clip(0.1 + 0.9 * jax.random.uniform(keys[2], (TOKENS, TOPK), jnp.float32) ** levels(keys[2], (TOKENS, TOPK), ((0, 32),), -0.2, 0.2), 0.1, 1.0)
    expert_ids = draw_expert_ids(jax.random.fold_in(keys[7], 71), 0)
    gate_weight = centred(keys[4], (D, EXP_WIN * FF), D ** -0.5, 0.09375, ((0, 32), (1, 32)))
    up_weight = centred(keys[5], (D, EXP_WIN * FF), D ** -0.5, 0.09375, ((0, 32), (1, 32)))
    down_weight = centred(keys[6], (EXP_WIN * FF, D), FF ** -0.5, 0.15625, ((0, 32), (1, 32)))
    return {"tokens": tokens, "out_grad": out_grad, "route_probs": route_probs, "expert_ids": expert_ids, "gate_weight": gate_weight, "up_weight": up_weight, "down_weight": down_weight}


def contract(left, right, left_dim, right_dim):
    return lax.dot_general(left, right, (((left_dim,), (right_dim,)), ((), ())), preferred_element_type=jnp.float32)


def select_rows(tok_group, grad_group, prob_group, ids_group, expert):
    hit = ids_group == expert
    weight = jnp.sum(jnp.where(hit, prob_group, jnp.zeros_like(prob_group)), axis=1)
    chosen = jnp.any(hit, axis=1)
    place = jnp.cumsum(chosen.astype(jnp.int32)) - 1
    slots = jnp.arange(CAP, dtype=jnp.int32)
    picker = chosen[None, :] & (place[None, :] == slots[:, None])
    pick_half = picker.astype(jnp.bfloat16)
    rows = jnp.dot(pick_half, tok_group, preferred_element_type=jnp.float32).astype(jnp.bfloat16)
    cot_rows = jnp.dot(pick_half, grad_group, preferred_element_type=jnp.float32).astype(jnp.bfloat16)
    row_weight = jnp.dot(picker.astype(jnp.float32), weight, precision=lax.Precision.HIGHEST)
    return pick_half, rows, cot_rows, row_weight


def reference(tokens, out_grad, route_probs, expert_ids, gate_weight, up_weight, down_weight):
    tok_all = tokens.reshape(N_FSDP, TOK_DEV, D)
    grad_all = out_grad.reshape(N_FSDP, TOK_DEV, D)
    prob_all = route_probs.reshape(N_FSDP, TOK_DEV, TOPK)
    ids_all = expert_ids.reshape(N_FSDP, TOK_DEV, TOPK)
    gate_pieces = gate_weight.reshape(D, N_EXPERT, HID_DEV).transpose(1, 0, 2)
    up_pieces = up_weight.reshape(D, N_EXPERT, HID_DEV).transpose(1, 0, 2)
    down_pieces = down_weight.reshape(N_EXPERT, HID_DEV, D)

    def one_piece(running, inputs):
        number, gate_w, up_w, down_w = inputs
        expert = number // SLICES

        def one_group(group):
            tok_group, grad_group, prob_group, ids_group = group
            pick_half, rows, cot_rows, row_weight = select_rows(tok_group, grad_group, prob_group, ids_group, expert)
            gate_value = jnp.dot(rows, gate_w, preferred_element_type=jnp.float32)
            up_value = jnp.dot(rows, up_w, preferred_element_type=jnp.float32)
            sigma = jax.nn.sigmoid(gate_value)
            active = gate_value * sigma
            hidden = (active * up_value).astype(jnp.bfloat16)
            carried = (row_weight[:, None] * cot_rows.astype(jnp.float32)).astype(jnp.bfloat16)
            hidden_grad = contract(carried, down_w, 1, 1)
            up_rows_grad = (hidden_grad * active).astype(jnp.bfloat16)
            gate_rows_grad = (hidden_grad * up_value * sigma * (1.0 + gate_value * (1.0 - sigma))).astype(jnp.bfloat16)
            row_grad = (contract(gate_rows_grad, gate_w, 1, 1) + contract(up_rows_grad, up_w, 1, 1)).astype(jnp.bfloat16)
            token_term = contract(pick_half, row_grad, 0, 0).astype(jnp.bfloat16)
            gate_term = contract(rows, gate_rows_grad, 0, 0).astype(jnp.bfloat16)
            up_term = contract(rows, up_rows_grad, 0, 0).astype(jnp.bfloat16)
            down_term = contract(hidden, carried, 0, 0).astype(jnp.bfloat16)
            return token_term, gate_term, up_term, down_term

        token_terms, gate_terms, up_terms, down_terms = lax.map(one_group, (tok_all, grad_all, prob_all, ids_all))
        sums = (jnp.sum(gate_terms.astype(jnp.float32), axis=0).astype(jnp.bfloat16),
                jnp.sum(up_terms.astype(jnp.float32), axis=0).astype(jnp.bfloat16),
                jnp.sum(down_terms.astype(jnp.float32), axis=0).astype(jnp.bfloat16))
        return running + token_terms.astype(jnp.float32), sums

    start = jnp.zeros((N_FSDP, TOK_DEV, D), jnp.float32)
    numbers = jnp.arange(N_EXPERT, dtype=jnp.int32)
    running, (gate_sums, up_sums, down_sums) = lax.scan(one_piece, start, (numbers, gate_pieces, up_pieces, down_pieces))
    x_grad = running.reshape(TOKENS, D).astype(jnp.bfloat16)
    gate_grad = gate_sums.transpose(1, 0, 2).reshape(D, N_EXPERT * HID_DEV)
    up_grad = up_sums.transpose(1, 0, 2).reshape(D, N_EXPERT * HID_DEV)
    down_grad = down_sums.reshape(N_EXPERT * HID_DEV, D)
    return x_grad, gate_grad, up_grad, down_grad
```

```python
import jax
import jax.numpy as jnp
from jax import lax
from jax.sharding import Mesh, PartitionSpec as P

CAP = 64
WINDOW = 4
SHAPE = (4, 2, 4, 4, 4, 2)
AXES = ("zp", "l", "x", "zh", "y", "c")
EXPERT = ("zp", "l", "x")
FSDP = ("zh", "y", "c")
PIECE = ("l", "x")
GROUP = ("y", "c")


def contract(left, right, left_dim, right_dim):
    return lax.dot_general(
        left, right, (((left_dim,), (right_dim,)), ((), ())), preferred_element_type=jnp.float32
    )


def gather(block, axis, size):
    copies = jnp.broadcast_to(block[None], (size,) + block.shape)
    return lax.all_to_all(copies, axis, 0, 0)


def exchange(blocks, axis):
    return lax.all_to_all(blocks, axis, 0, 0)


def swap(block):
    pairs = [(piece * 8 + group, group * 8 + piece) for piece in range(8) for group in range(8)]
    return lax.ppermute(block, PIECE + GROUP, pairs)


def select(probs, ids):
    window = jnp.arange(WINDOW, dtype=jnp.int32)
    hit = ids[None] == window[:, None, None]
    weight = jnp.sum(jnp.where(hit, probs[None], 0.0), axis=2)
    chosen = jnp.any(hit, axis=2)
    count = ids.shape[0]
    before = jnp.arange(count)[:, None] <= jnp.arange(count)[None, :]
    place = jnp.dot(
        chosen.astype(jnp.bfloat16), before.astype(jnp.bfloat16), preferred_element_type=jnp.float32
    ).astype(jnp.int32)
    slots = jnp.arange(1, CAP + 1, dtype=jnp.int32)
    picker = chosen[:, None, :] & (place[:, None, :] == slots[None, :, None])
    row_weight = jnp.sum(jnp.where(picker, weight[:, None, :], 0.0), axis=2)
    return picker.reshape(WINDOW * CAP, count).astype(jnp.bfloat16), row_weight.reshape(-1)


def shards(tokens, out_grad, route_probs, expert_ids, gate_weight, up_weight, down_weight):
    hid, feat = down_weight.shape
    own = jnp.concatenate([gate_weight.T, up_weight.T, down_weight], axis=0)
    weights = gather(own, "zh", 4).transpose(1, 0, 2).reshape(3 * hid, 4 * feat)
    gate_up, down = weights[: 2 * hid], weights[2 * hid :]

    picker, row_weight = select(route_probs, expert_ids)
    picked = jnp.dot(picker, tokens, preferred_element_type=jnp.float32).astype(jnp.bfloat16)
    cot_rows = jnp.dot(picker, out_grad, preferred_element_type=jnp.float32)
    carried = (row_weight[:, None] * cot_rows).astype(jnp.bfloat16)
    both = jnp.stack([picked, carried]).reshape(2, WINDOW, CAP, feat).transpose(1, 2, 0, 3)
    both = exchange(both.reshape(WINDOW, CAP, 2 * feat), "zp")
    both = both.reshape(4, CAP, 2, feat).transpose(1, 2, 0, 3).reshape(CAP, 8 * feat)
    both = gather(swap(both), PIECE, 8).reshape(8 * CAP, 8 * feat)
    rows, carried = both[:, : 4 * feat], both[:, 4 * feat :]

    parts = jnp.concatenate(
        [contract(rows, gate_up, 1, 1), contract(carried, down, 1, 1)], axis=1
    ).astype(jnp.bfloat16)
    values = jnp.sum(
        exchange(parts.reshape(8, CAP, 3 * hid), GROUP).astype(jnp.float32), axis=0
    )
    gate_value, up_value, hidden_grad = (
        values[:, :hid],
        values[:, hid : 2 * hid],
        values[:, 2 * hid :],
    )
    sigma = jax.nn.sigmoid(gate_value)
    active = gate_value * sigma
    hidden = (active * up_value).astype(jnp.bfloat16)
    up_rows_grad = (hidden_grad * active).astype(jnp.bfloat16)
    gate_rows_grad = (hidden_grad * up_value * sigma * (1.0 + gate_value * (1.0 - sigma))).astype(
        jnp.bfloat16
    )
    acts = jnp.concatenate([gate_rows_grad, up_rows_grad, hidden], axis=1)
    acts = gather(acts, GROUP, 8).reshape(8 * CAP, 3 * hid)
    row_grads, hidden = acts[:, : 2 * hid], acts[:, 2 * hid :]

    terms = jnp.concatenate(
        [contract(row_grads, rows, 0, 0), contract(hidden, carried, 0, 0)], axis=0
    ).astype(jnp.bfloat16)
    summed = exchange(terms.reshape(3 * hid, 4, feat).transpose(1, 0, 2), "zh")
    summed = jnp.sum(summed.astype(jnp.float32), axis=0).astype(jnp.bfloat16)
    gate_grad, up_grad = summed[:hid].T, summed[hid : 2 * hid].T
    down_grad = summed[2 * hid :]

    row_grad = contract(row_grads, gate_up, 1, 0).astype(jnp.bfloat16).reshape(8, CAP, 4 * feat)
    row_grad = exchange(row_grad, PIECE).astype(jnp.float32)
    row_grad = swap(jnp.sum(row_grad, axis=0).astype(jnp.bfloat16))
    row_grad = exchange(row_grad.reshape(CAP, 4, feat).transpose(1, 0, 2), "zp")
    x_grad = contract(picker, row_grad.reshape(WINDOW * CAP, feat), 0, 0).astype(jnp.bfloat16)
    return (x_grad, gate_grad, up_grad, down_grad)


def solution(mesh):
    fine = Mesh(mesh.devices.reshape(SHAPE), AXES)
    placed = (
        P(FSDP, EXPERT),
        P(FSDP, EXPERT),
        P(FSDP, None),
        P(FSDP, None),
        P(FSDP, EXPERT),
        P(FSDP, EXPERT),
        P(EXPERT, FSDP),
    )
    return jax.shard_map(
        shards,
        mesh=fine,
        in_specs=placed,
        out_specs=(P(FSDP, EXPERT), P(FSDP, EXPERT), P(FSDP, EXPERT), P(EXPERT, FSDP)),
        check_vma=False,
    )
```

```python
import jax
import jax.numpy as jnp
from jax import lax
from jax.sharding import Mesh, PartitionSpec as P

CAP = 64
WINDOW = 4
SHAPE = (4, 2, 4, 4, 4, 2)
AXES = ("zp", "l", "x", "zh", "y", "c")
EXPERT = ("zp", "l", "x")
FSDP = ("zh", "y", "c")
PIECE = ("l", "x")
GROUP = ("y", "c")


def contract(left, right, left_dim, right_dim):
    return lax.dot_general(
        left, right, (((left_dim,), (right_dim,)), ((), ())), preferred_element_type=jnp.float32
    )


def gather(block, axis, size):
    copies = jnp.broadcast_to(block[None], (size,) + block.shape)
    return lax.all_to_all(copies, axis, 0, 0)


def exchange(blocks, axis):
    return lax.all_to_all(blocks, axis, 0, 0)


def swap(block):
    pairs = [(piece * 8 + group, group * 8 + piece) for piece in range(8) for group in range(8)]
    return lax.ppermute(block, PIECE + GROUP, pairs)


def select(probs, ids):
    window = jnp.arange(WINDOW, dtype=jnp.int32)
    hit = ids[None] == window[:, None, None]
    weight = jnp.sum(jnp.where(hit, probs[None], 0.0), axis=2)
    chosen = jnp.any(hit, axis=2)
    count = ids.shape[0]
    before = jnp.arange(count)[:, None] <= jnp.arange(count)[None, :]
    place = jnp.dot(
        chosen.astype(jnp.bfloat16), before.astype(jnp.bfloat16), preferred_element_type=jnp.float32
    ).astype(jnp.int32)
    slots = jnp.arange(1, CAP + 1, dtype=jnp.int32)
    picker = chosen[:, None, :] & (place[:, None, :] == slots[None, :, None])
    row_weight = jnp.sum(jnp.where(picker, weight[:, None, :], 0.0), axis=2)
    return picker.reshape(WINDOW * CAP, count).astype(jnp.bfloat16), row_weight.reshape(-1)


def shards(tokens, out_grad, route_probs, expert_ids, gate_weight, up_weight, down_weight):
    hid, feat = down_weight.shape
    picker, row_weight = select(route_probs, expert_ids)
    picked = jnp.dot(picker, tokens, preferred_element_type=jnp.float32).astype(jnp.bfloat16)
    cot_rows = jnp.dot(picker, out_grad, preferred_element_type=jnp.float32)
    carried = (row_weight[:, None] * cot_rows).astype(jnp.bfloat16)
    both = jnp.stack([picked, carried]).reshape(2, WINDOW, CAP, feat).transpose(1, 2, 0, 3)
    both = exchange(both.reshape(WINDOW, CAP, 2 * feat), "zp")

    own = jnp.concatenate([gate_weight.T, up_weight.T, down_weight], axis=0)
    own, both = lax.optimization_barrier((own, both))
    weights = lax.all_gather(own, "zh").transpose(1, 0, 2).reshape(3 * hid, 4 * feat)
    gate_up, down = weights[: 2 * hid], weights[2 * hid :]

    both = both.reshape(4, CAP, 2, feat).transpose(1, 2, 0, 3).reshape(CAP, 8 * feat)
    both = gather(swap(both), PIECE, 8).reshape(8 * CAP, 8 * feat)
    rows, carried = both[:, : 4 * feat], both[:, 4 * feat :]

    parts = jnp.concatenate(
        [contract(rows, gate_up, 1, 1), contract(carried, down, 1, 1)], axis=1
    ).astype(jnp.bfloat16)
    values = jnp.sum(
        exchange(parts.reshape(8, CAP, 3 * hid), GROUP).astype(jnp.float32), axis=0
    )
    gate_value, up_value, hidden_grad = (
        values[:, :hid],
        values[:, hid : 2 * hid],
        values[:, 2 * hid :],
    )
    sigma = jax.nn.sigmoid(gate_value)
    active = gate_value * sigma
    hidden = (active * up_value).astype(jnp.bfloat16)
    up_rows_grad = (hidden_grad * active).astype(jnp.bfloat16)
    gate_rows_grad = (hidden_grad * up_value * sigma * (1.0 + gate_value * (1.0 - sigma))).astype(
        jnp.bfloat16
    )
    acts = jnp.concatenate([gate_rows_grad, up_rows_grad, hidden], axis=1)
    acts = gather(acts, GROUP, 8).reshape(8 * CAP, 3 * hid)
    row_grads, hidden = acts[:, : 2 * hid], acts[:, 2 * hid :]

    terms = jnp.concatenate(
        [contract(row_grads, rows, 0, 0), contract(hidden, carried, 0, 0)], axis=0
    ).astype(jnp.bfloat16)
    terms, row_grads = lax.optimization_barrier(
        (terms.reshape(3 * hid, 4, feat).transpose(1, 0, 2), row_grads)
    )
    summed = lax.psum_scatter(terms, "zh")
    gate_grad, up_grad = summed[:hid].T, summed[hid : 2 * hid].T
    down_grad = summed[2 * hid :]

    row_grad = contract(row_grads, gate_up, 1, 0).astype(jnp.bfloat16).reshape(8, CAP, 4 * feat)
    row_grad = exchange(row_grad, PIECE).astype(jnp.float32)
    row_grad = swap(jnp.sum(row_grad, axis=0).astype(jnp.bfloat16))
    row_grad = exchange(row_grad.reshape(CAP, 4, feat).transpose(1, 0, 2), "zp")
    x_grad = contract(picker, row_grad.reshape(WINDOW * CAP, feat), 0, 0).astype(jnp.bfloat16)
    return (x_grad, gate_grad, up_grad, down_grad)


def solution(mesh):
    fine = Mesh(mesh.devices.reshape(SHAPE), AXES)
    placed = (
        P(FSDP, EXPERT),
        P(FSDP, EXPERT),
        P(FSDP, None),
        P(FSDP, None),
        P(FSDP, EXPERT),
        P(FSDP, EXPERT),
        P(EXPERT, FSDP),
    )
    return jax.shard_map(
        shards,
        mesh=fine,
        in_specs=placed,
        out_specs=(P(FSDP, EXPERT), P(FSDP, EXPERT), P(FSDP, EXPERT), P(EXPERT, FSDP)),
        check_vma=False,
    )
```

```python
import jax
import jax.numpy as jnp
from jax import lax
from jax.sharding import Mesh, PartitionSpec as P

CAP = 64
WINDOW = 4
SHAPE = (4, 2, 4, 4, 4, 2)
AXES = ("zp", "l", "x", "zh", "y", "c")
EXPERT = ("zp", "l", "x")
FSDP = ("zh", "y", "c")
PIECE = ("l", "x")
GROUP = ("y", "c")


def contract(left, right, left_dim, right_dim):
    return lax.dot_general(
        left, right, (((left_dim,), (right_dim,)), ((), ())), preferred_element_type=jnp.float32
    )


def gather(block, axis, size):
    copies = jnp.broadcast_to(block[None], (size,) + block.shape)
    return lax.all_to_all(copies, axis, 0, 0)


def exchange(blocks, axis):
    return lax.all_to_all(blocks, axis, 0, 0)


def swap(block):
    pairs = [(piece * 8 + group, group * 8 + piece) for piece in range(8) for group in range(8)]
    return lax.ppermute(block, PIECE + GROUP, pairs)


def select(probs, ids):
    window = jnp.arange(WINDOW, dtype=jnp.int32)
    hit = ids[None] == window[:, None, None]
    weight = jnp.sum(jnp.where(hit, probs[None], 0.0), axis=2)
    chosen = jnp.any(hit, axis=2)
    count = ids.shape[0]
    before = jnp.arange(count)[:, None] <= jnp.arange(count)[None, :]
    place = jnp.dot(
        chosen.astype(jnp.bfloat16), before.astype(jnp.bfloat16), preferred_element_type=jnp.float32
    ).astype(jnp.int32)
    slots = jnp.arange(1, CAP + 1, dtype=jnp.int32)
    picker = chosen[:, None, :] & (place[:, None, :] == slots[None, :, None])
    row_weight = jnp.sum(jnp.where(picker, weight[:, None, :], 0.0), axis=2)
    return picker.reshape(WINDOW * CAP, count).astype(jnp.bfloat16), row_weight.reshape(-1)


def once(step, value, out_shape):
    turns = 1 + lax.axis_index("x") // 4
    start = (jnp.int32(0), value, jnp.zeros(out_shape, jnp.bfloat16))
    return lax.while_loop(
        lambda state: state[0] < turns,
        lambda state: (state[0] + 1, state[1], step(state[1] + state[0].astype(jnp.bfloat16))),
        start,
    )[2]


def turned(blocks):
    here = lax.axis_index("zh")
    return jnp.stack(
        [lax.dynamic_index_in_dim(blocks, (here - d) % 4, 0, False) for d in range(4)]
    )


def token_chain(both):
    both = turned(exchange(both, "zp"))
    feat = both.shape[2] // 2
    both = both.reshape(4, CAP, 2, feat).transpose(1, 2, 0, 3).reshape(CAP, 8 * feat)
    return gather(swap(both), PIECE, 8).reshape(8 * CAP, 8 * feat)


def grad_chain(row_grad):
    feat = row_grad.shape[2] // 4
    row_grad = exchange(row_grad, PIECE).astype(jnp.float32)
    row_grad = swap(jnp.sum(row_grad, axis=0).astype(jnp.bfloat16))
    return exchange(turned(row_grad.reshape(CAP, 4, feat).transpose(1, 0, 2)), "zp")


def shift(block, d):
    return lax.ppermute(block, "zh", [(j, (j + d) % 4) for j in range(4)])


def shards(tokens, out_grad, route_probs, expert_ids, gate_weight, up_weight, down_weight):
    hid, feat = down_weight.shape
    own = jnp.concatenate([gate_weight.T, up_weight.T, down_weight], axis=0)
    moved = [shift(own, d) for d in (1, 2, 3)]

    picker, row_weight = select(route_probs, expert_ids)
    picked = jnp.dot(picker, tokens, preferred_element_type=jnp.float32).astype(jnp.bfloat16)
    cot_rows = jnp.dot(picker, out_grad, preferred_element_type=jnp.float32)
    carried = (row_weight[:, None] * cot_rows).astype(jnp.bfloat16)
    both = jnp.concatenate([picked, carried], axis=1).reshape(WINDOW, CAP, 2 * feat)
    both = once(token_chain, both, (8 * CAP, 8 * feat))
    rows, carried = both[:, : 4 * feat], both[:, 4 * feat :]
    weights = jnp.concatenate([own] + moved, axis=1) + both[:1, :1] * 0
    gate_up, down = weights[: 2 * hid], weights[2 * hid :]

    parts = jnp.concatenate(
        [contract(rows, gate_up, 1, 1), contract(carried, down, 1, 1)], axis=1
    ).astype(jnp.bfloat16)
    values = jnp.sum(
        exchange(parts.reshape(8, CAP, 3 * hid), GROUP).astype(jnp.float32), axis=0
    )
    gate_value, up_value, hidden_grad = (
        values[:, :hid],
        values[:, hid : 2 * hid],
        values[:, 2 * hid :],
    )
    sigma = jax.nn.sigmoid(gate_value)
    active = gate_value * sigma
    hidden = (active * up_value).astype(jnp.bfloat16)
    up_rows_grad = (hidden_grad * active).astype(jnp.bfloat16)
    gate_rows_grad = (hidden_grad * up_value * sigma * (1.0 + gate_value * (1.0 - sigma))).astype(
        jnp.bfloat16
    )
    acts = jnp.concatenate([gate_rows_grad, up_rows_grad, hidden], axis=1)
    acts = gather(acts, GROUP, 8).reshape(8 * CAP, 3 * hid)
    row_grads, hidden = acts[:, : 2 * hid], acts[:, 2 * hid :]

    terms = jnp.concatenate(
        [contract(row_grads, rows, 0, 0), contract(hidden, carried, 0, 0)], axis=0
    ).astype(jnp.bfloat16)
    terms = [terms[:, d * feat : (d + 1) * feat] for d in range(4)]
    moved = [shift(terms[d], -d) for d in (1, 2, 3)]
    row_grad = contract(row_grads, gate_up, 1, 0).astype(jnp.bfloat16).reshape(8, CAP, 4 * feat)
    row_grad = once(grad_chain, row_grad, (WINDOW, CAP, feat))
    summed = terms[0].astype(jnp.float32) + row_grad[0, :1, :1].astype(jnp.float32) * 0
    for d in (1, 2, 3):
        summed = summed + moved[d - 1].astype(jnp.float32)
    summed = summed.astype(jnp.bfloat16)
    gate_grad, up_grad = summed[:hid].T, summed[hid : 2 * hid].T
    down_grad = summed[2 * hid :]

    x_grad = contract(picker, row_grad.reshape(WINDOW * CAP, feat), 0, 0).astype(jnp.bfloat16)
    return (x_grad, gate_grad, up_grad, down_grad)


def solution(mesh):
    fine = Mesh(mesh.devices.reshape(SHAPE), AXES)
    placed = (
        P(FSDP, EXPERT),
        P(FSDP, EXPERT),
        P(FSDP, None),
        P(FSDP, None),
        P(FSDP, EXPERT),
        P(FSDP, EXPERT),
        P(EXPERT, FSDP),
    )
    return jax.shard_map(
        shards,
        mesh=fine,
        in_specs=placed,
        out_specs=(P(FSDP, EXPERT), P(FSDP, EXPERT), P(FSDP, EXPERT), P(EXPERT, FSDP)),
        check_vma=False,
    )
```

```python
import jax
import jax.numpy as jnp
from jax import lax
from jax.sharding import Mesh, PartitionSpec as P

CAP = 64
WINDOW = 4
SHAPE = (4, 2, 4, 4, 4, 2)
AXES = ("zp", "l", "x", "zh", "y", "c")
EXPERT = ("zp", "l", "x")
FSDP = ("zh", "y", "c")
PIECE = ("l", "x")
GROUP = ("y", "c")


def contract(left, right, left_dim, right_dim):
    return lax.dot_general(
        left, right, (((left_dim,), (right_dim,)), ((), ())), preferred_element_type=jnp.float32
    )


def gather(block, axis, size):
    copies = jnp.broadcast_to(block[None], (size,) + block.shape)
    return lax.all_to_all(copies, axis, 0, 0)


def exchange(blocks, axis):
    return lax.all_to_all(blocks, axis, 0, 0)


def swap(block):
    pairs = [(piece * 8 + group, group * 8 + piece) for piece in range(8) for group in range(8)]
    return lax.ppermute(block, PIECE + GROUP, pairs)


def select(probs, ids):
    window = jnp.arange(WINDOW, dtype=jnp.int32)
    hit = ids[None] == window[:, None, None]
    weight = jnp.sum(jnp.where(hit, probs[None], 0.0), axis=2)
    chosen = jnp.any(hit, axis=2)
    count = ids.shape[0]
    before = jnp.arange(count)[:, None] <= jnp.arange(count)[None, :]
    place = jnp.dot(
        chosen.astype(jnp.bfloat16), before.astype(jnp.bfloat16), preferred_element_type=jnp.float32
    ).astype(jnp.int32)
    slots = jnp.arange(1, CAP + 1, dtype=jnp.int32)
    picker = chosen[:, None, :] & (place[:, None, :] == slots[None, :, None])
    row_weight = jnp.sum(jnp.where(picker, weight[:, None, :], 0.0), axis=2)
    return picker.reshape(WINDOW * CAP, count).astype(jnp.bfloat16), row_weight.reshape(-1)


def once(step, value, out_shape):
    turns = 1 + lax.axis_index("x") // 4
    start = (jnp.int32(0), value, jnp.zeros(out_shape, jnp.bfloat16))
    return lax.while_loop(
        lambda state: state[0] < turns,
        lambda state: (state[0] + 1, state[1], step(state[1] + state[0].astype(jnp.bfloat16))),
        start,
    )[2]


def token_chain(both):
    both = exchange(both, "zp")
    feat = both.shape[2] // 2
    both = both.reshape(4, CAP, 2, feat).transpose(1, 2, 0, 3).reshape(CAP, 8 * feat)
    return gather(swap(both), PIECE, 8).reshape(8 * CAP, 8 * feat)


def grad_chain(row_grad):
    feat = row_grad.shape[2] // 4
    row_grad = exchange(row_grad, PIECE).astype(jnp.float32)
    row_grad = swap(jnp.sum(row_grad, axis=0).astype(jnp.bfloat16))
    return exchange(row_grad.reshape(CAP, 4, feat).transpose(1, 0, 2), "zp")


def shards(tokens, out_grad, route_probs, expert_ids, gate_weight, up_weight, down_weight):
    hid, feat = down_weight.shape
    own = jnp.concatenate([gate_weight.T, up_weight.T, down_weight], axis=0)
    weights = lax.all_gather(own, ("zh", "c")).reshape(4, 2, 3 * hid, feat)

    picker, row_weight = select(route_probs, expert_ids)
    picked = jnp.dot(picker, tokens, preferred_element_type=jnp.float32).astype(jnp.bfloat16)
    cot_rows = jnp.dot(picker, out_grad, preferred_element_type=jnp.float32)
    carried = (row_weight[:, None] * cot_rows).astype(jnp.bfloat16)
    both = jnp.concatenate([picked, carried], axis=1).reshape(WINDOW, CAP, 2 * feat)
    both = once(token_chain, both, (8 * CAP, 8 * feat))
    rows, carried = both[:, : 4 * feat], both[:, 4 * feat :]
    weights = lax.dynamic_index_in_dim(weights, lax.axis_index("c"), 1, False)
    weights = jnp.concatenate(list(weights), axis=1) + both[:1, :1] * 0
    gate_up, down = weights[: 2 * hid], weights[2 * hid :]

    parts = jnp.concatenate(
        [contract(rows, gate_up, 1, 1), contract(carried, down, 1, 1)], axis=1
    ).astype(jnp.bfloat16)
    values = jnp.sum(
        exchange(parts.reshape(8, CAP, 3 * hid), GROUP).astype(jnp.float32), axis=0
    )
    gate_value, up_value, hidden_grad = (
        values[:, :hid],
        values[:, hid : 2 * hid],
        values[:, 2 * hid :],
    )
    sigma = jax.nn.sigmoid(gate_value)
    active = gate_value * sigma
    hidden = (active * up_value).astype(jnp.bfloat16)
    up_rows_grad = (hidden_grad * active).astype(jnp.bfloat16)
    gate_rows_grad = (hidden_grad * up_value * sigma * (1.0 + gate_value * (1.0 - sigma))).astype(
        jnp.bfloat16
    )
    acts = jnp.concatenate([gate_rows_grad, up_rows_grad, hidden], axis=1)
    acts = gather(acts, GROUP, 8).reshape(8 * CAP, 3 * hid)
    row_grads, hidden = acts[:, : 2 * hid], acts[:, 2 * hid :]

    terms = jnp.concatenate(
        [contract(row_grads, rows, 0, 0), contract(hidden, carried, 0, 0)], axis=0
    ).astype(jnp.bfloat16)
    summed = lax.psum_scatter(terms.reshape(3 * hid, 4, feat).transpose(1, 0, 2), "zh")
    row_grad = contract(row_grads, gate_up, 1, 0).astype(jnp.bfloat16).reshape(8, CAP, 4 * feat)
    row_grad = once(grad_chain, row_grad, (WINDOW, CAP, feat))
    summed = summed + row_grad[0, :1, :1] * 0
    gate_grad, up_grad = summed[:hid].T, summed[hid : 2 * hid].T
    down_grad = summed[2 * hid :]

    x_grad = contract(picker, row_grad.reshape(WINDOW * CAP, feat), 0, 0).astype(jnp.bfloat16)
    return (x_grad, gate_grad, up_grad, down_grad)


def solution(mesh):
    fine = Mesh(mesh.devices.reshape(SHAPE), AXES)
    placed = (
        P(FSDP, EXPERT),
        P(FSDP, EXPERT),
        P(FSDP, None),
        P(FSDP, None),
        P(FSDP, EXPERT),
        P(FSDP, EXPERT),
        P(EXPERT, FSDP),
    )
    return jax.shard_map(
        shards,
        mesh=fine,
        in_specs=placed,
        out_specs=(P(FSDP, EXPERT), P(FSDP, EXPERT), P(FSDP, EXPERT), P(EXPERT, FSDP)),
        check_vma=False,
    )
```

```python
import jax
import jax.numpy as jnp
from jax import lax
from jax.sharding import Mesh, PartitionSpec as P

CAP = 64
WINDOW = 4
SHAPE = (4, 2, 4, 4, 2, 2, 2)
AXES = ("zp", "l", "x", "zh", "y_high", "y_low", "c")
EXPERT = ("zp", "l", "x")
FSDP = ("zh", "y_high", "y_low", "c")
PIECE = ("x", "l")
GROUP = ("y_low", "c", "y_high")


def contract(left, right, left_dim, right_dim):
    return lax.dot_general(
        left, right, (((left_dim,), (right_dim,)), ((), ())), preferred_element_type=jnp.float32
    )


def gather(block, axis, size):
    copies = jnp.broadcast_to(block[None], (size,) + block.shape)
    return lax.all_to_all(copies, axis, 0, 0)


def exchange(blocks, axis):
    return lax.all_to_all(blocks, axis, 0, 0)


def swap(block, flip=0):
    pairs = [
        (piece * 8 + group, (group ^ flip) * 8 + piece) for piece in range(8) for group in range(8)
    ]
    return lax.ppermute(block, ("l", "x", "y_high", "y_low", "c"), pairs)


def select(probs, ids):
    window = jnp.arange(WINDOW, dtype=jnp.int32)
    hit = ids[None] == window[:, None, None]
    weight = jnp.sum(jnp.where(hit, probs[None], 0.0), axis=2)
    chosen = jnp.any(hit, axis=2)
    count = ids.shape[0]
    before = jnp.arange(count)[:, None] <= jnp.arange(count)[None, :]
    place = jnp.dot(
        chosen.astype(jnp.bfloat16), before.astype(jnp.bfloat16), preferred_element_type=jnp.float32
    ).astype(jnp.int32)
    slots = jnp.arange(1, CAP + 1, dtype=jnp.int32)
    picker = chosen[:, None, :] & (place[:, None, :] == slots[None, :, None])
    row_weight = jnp.sum(jnp.where(picker, weight[:, None, :], 0.0), axis=2)
    return picker.reshape(WINDOW * CAP, count).astype(jnp.bfloat16), row_weight.reshape(-1)


def once(step, value, out_shape):
    turns = 1 + lax.axis_index("x") // 4
    start = (jnp.int32(0), value, jnp.zeros(out_shape, jnp.bfloat16))
    return lax.while_loop(
        lambda state: state[0] < turns,
        lambda state: (state[0] + 1, state[1], step(state[1] + state[0].astype(jnp.bfloat16))),
        start,
    )[2]


def token_chain(both):
    both = exchange(both, "zp")
    feat = both.shape[2] // 2
    both = both.reshape(4, CAP, 2, feat).transpose(1, 2, 0, 3).reshape(CAP, 8 * feat)
    same, other = swap(both), swap(both, 4)
    low = lax.axis_index("l") == 0
    both = jnp.stack([jnp.where(low, same, other), jnp.where(low, other, same)])
    return gather(both, "x", 4).reshape(8 * CAP, 8 * feat)


def grad_chain(row_grad):
    feat = row_grad.shape[2] // 4
    row_grad = exchange(row_grad, PIECE).astype(jnp.float32)
    row_grad = swap(jnp.sum(row_grad, axis=0).astype(jnp.bfloat16))
    return exchange(row_grad.reshape(CAP, 4, feat).transpose(1, 0, 2), "zp")


def shards(tokens, out_grad, route_probs, expert_ids, gate_weight, up_weight, down_weight):
    hid, feat = down_weight.shape
    own = jnp.concatenate([gate_weight.T, up_weight.T, down_weight], axis=0)
    weights = lax.all_gather(own, ("zh", "c")).reshape(4, 2, 3 * hid, feat)

    picker, row_weight = select(route_probs, expert_ids)
    picked = jnp.dot(picker, tokens, preferred_element_type=jnp.float32).astype(jnp.bfloat16)
    cot_rows = jnp.dot(picker, out_grad, preferred_element_type=jnp.float32)
    carried = (row_weight[:, None] * cot_rows).astype(jnp.bfloat16)
    both = jnp.concatenate([picked, carried], axis=1).reshape(WINDOW, CAP, 2 * feat)
    both = once(token_chain, both, (8 * CAP, 8 * feat))
    rows, carried = both[:, : 4 * feat], both[:, 4 * feat :]
    weights = lax.dynamic_index_in_dim(weights, lax.axis_index("c"), 1, False)
    weights = jnp.concatenate(list(weights), axis=1) + both[:1, :1] * 0
    gate_up, down = weights[: 2 * hid], weights[2 * hid :]

    parts = jnp.concatenate(
        [contract(rows, gate_up, 1, 1), contract(carried, down, 1, 1)], axis=1
    ).astype(jnp.bfloat16)
    values = jnp.sum(
        exchange(parts.reshape(8, CAP, 3 * hid), GROUP).astype(jnp.float32), axis=0
    )
    gate_value, up_value, hidden_grad = (
        values[:, :hid],
        values[:, hid : 2 * hid],
        values[:, 2 * hid :],
    )
    sigma = jax.nn.sigmoid(gate_value)
    active = gate_value * sigma
    hidden = (active * up_value).astype(jnp.bfloat16)
    up_rows_grad = (hidden_grad * active).astype(jnp.bfloat16)
    gate_rows_grad = (hidden_grad * up_value * sigma * (1.0 + gate_value * (1.0 - sigma))).astype(
        jnp.bfloat16
    )
    acts = jnp.concatenate([gate_rows_grad, up_rows_grad, hidden], axis=1)
    acts = gather(acts, GROUP, 8).reshape(8 * CAP, 3 * hid)
    row_grads, hidden = acts[:, : 2 * hid], acts[:, 2 * hid :]

    terms = jnp.concatenate(
        [contract(row_grads, rows, 0, 0), contract(hidden, carried, 0, 0)], axis=0
    ).astype(jnp.bfloat16)
    summed = lax.psum_scatter(terms.reshape(3 * hid, 4, feat).transpose(1, 0, 2), "zh")
    row_grad = contract(row_grads, gate_up, 1, 0).astype(jnp.bfloat16).reshape(8, CAP, 4 * feat)
    row_grad = once(grad_chain, row_grad, (WINDOW, CAP, feat))
    summed = summed + row_grad[0, :1, :1] * 0
    gate_grad, up_grad = summed[:hid].T, summed[hid : 2 * hid].T
    down_grad = summed[2 * hid :]

    x_grad = contract(picker, row_grad.reshape(WINDOW * CAP, feat), 0, 0).astype(jnp.bfloat16)
    return (x_grad, gate_grad, up_grad, down_grad)


def solution(mesh):
    fine = Mesh(mesh.devices.reshape(SHAPE), AXES)
    placed = (
        P(FSDP, EXPERT),
        P(FSDP, EXPERT),
        P(FSDP, None),
        P(FSDP, None),
        P(FSDP, EXPERT),
        P(FSDP, EXPERT),
        P(EXPERT, FSDP),
    )
    return jax.shard_map(
        shards,
        mesh=fine,
        in_specs=placed,
        out_specs=(P(FSDP, EXPERT), P(FSDP, EXPERT), P(FSDP, EXPERT), P(EXPERT, FSDP)),
        check_vma=False,
    )
```

```python
import jax
import jax.numpy as jnp
from jax import lax
from jax.sharding import Mesh, PartitionSpec as P

CAP = 64
WINDOW = 4
SHAPE = (4, 2, 4, 4, 2, 2, 2)
AXES = ("zp", "l", "x", "zh", "y_high", "y_low", "c")
EXPERT = ("zp", "l", "x")
FSDP = ("zh", "y_high", "y_low", "c")
PIECE = ("x", "l")
GROUP = ("y_low", "c", "y_high")


def contract(left, right, left_dim, right_dim):
    return lax.dot_general(
        left, right, (((left_dim,), (right_dim,)), ((), ())), preferred_element_type=jnp.float32
    )


def gather(block, axis, size):
    copies = jnp.broadcast_to(block[None], (size,) + block.shape)
    return lax.all_to_all(copies, axis, 0, 0)


def exchange(blocks, axis):
    return lax.all_to_all(blocks, axis, 0, 0)


def swap(block, piece_flip=0, group_flip=0):
    pairs = [
        (piece * 8 + group, (group ^ piece_flip) * 8 + (piece ^ group_flip))
        for piece in range(8)
        for group in range(8)
    ]
    return lax.ppermute(block, ("l", "x", "y_high", "y_low", "c"), pairs)


def select(probs, ids):
    window = jnp.arange(WINDOW, dtype=jnp.int32)
    hit = ids[None] == window[:, None, None]
    weight = jnp.sum(jnp.where(hit, probs[None], 0.0), axis=2)
    chosen = jnp.any(hit, axis=2)
    count = ids.shape[0]
    before = jnp.arange(count)[:, None] <= jnp.arange(count)[None, :]
    place = jnp.dot(
        chosen.astype(jnp.bfloat16), before.astype(jnp.bfloat16), preferred_element_type=jnp.float32
    ).astype(jnp.int32)
    slots = jnp.arange(1, CAP + 1, dtype=jnp.int32)
    picker = chosen[:, None, :] & (place[:, None, :] == slots[None, :, None])
    row_weight = jnp.sum(jnp.where(picker, weight[:, None, :], 0.0), axis=2)
    return picker.reshape(WINDOW * CAP, count).astype(jnp.bfloat16), row_weight.reshape(-1)


def once(step, value, out_shape):
    turns = 1 + lax.axis_index("x") // 4
    start = (jnp.int32(0), value, jnp.zeros(out_shape, jnp.bfloat16))
    return lax.while_loop(
        lambda state: state[0] < turns,
        lambda state: (state[0] + 1, state[1], step(state[1] + state[0].astype(jnp.bfloat16))),
        start,
    )[2]


def ordered(same, other):
    low = lax.axis_index("l") == 0
    return jnp.where(low, same, other), jnp.where(low, other, same)


def token_chain(both):
    both = exchange(both, "zp")
    feat = both.shape[2] // 2
    both = both.reshape(4, CAP, 2, feat).transpose(1, 2, 0, 3).reshape(CAP, 8 * feat)
    both = jnp.stack(ordered(swap(both), swap(both, piece_flip=4)))
    return gather(both, "x", 4).reshape(8 * CAP, 8 * feat)


def grad_chain(row_grad):
    feat = row_grad.shape[3] // 4
    row_grad = jnp.sum(exchange(row_grad, "x").astype(jnp.float32), axis=0).astype(jnp.bfloat16)
    same, other = ordered(row_grad[0], row_grad[1])
    same, other = swap(same), swap(other, group_flip=4)
    row_grad = (same.astype(jnp.float32) + other.astype(jnp.float32)).astype(jnp.bfloat16)
    return exchange(row_grad.reshape(CAP, 4, feat).transpose(1, 0, 2), "zp")


def shift(block, d):
    return lax.ppermute(block, "zh", [(j, (j + d) % 4) for j in range(4)])


def shards(tokens, out_grad, route_probs, expert_ids, gate_weight, up_weight, down_weight):
    hid, feat = down_weight.shape
    own = jnp.concatenate([gate_weight.T, up_weight.T, down_weight], axis=0)
    weights = lax.all_gather(own, "zh")
    weights = jnp.concatenate(list(weights), axis=1)
    gate_up, down = weights[: 2 * hid], weights[2 * hid :]

    picker, row_weight = select(route_probs, expert_ids)
    picked = jnp.dot(picker, tokens, preferred_element_type=jnp.float32).astype(jnp.bfloat16)
    cot_rows = jnp.dot(picker, out_grad, preferred_element_type=jnp.float32)
    carried = (row_weight[:, None] * cot_rows).astype(jnp.bfloat16)
    both = jnp.concatenate([picked, carried], axis=1).reshape(WINDOW, CAP, 2 * feat)
    both = token_chain(both)
    rows, carried = both[:, : 4 * feat], both[:, 4 * feat :]

    parts = jnp.concatenate(
        [contract(rows, gate_up, 1, 1), contract(carried, down, 1, 1)], axis=1
    ).astype(jnp.bfloat16)
    values = jnp.sum(
        exchange(parts.reshape(8, CAP, 3 * hid), GROUP).astype(jnp.float32), axis=0
    )
    gate_value, up_value, hidden_grad = (
        values[:, :hid],
        values[:, hid : 2 * hid],
        values[:, 2 * hid :],
    )
    sigma = jax.nn.sigmoid(gate_value)
    active = gate_value * sigma
    hidden = (active * up_value).astype(jnp.bfloat16)
    up_rows_grad = (hidden_grad * active).astype(jnp.bfloat16)
    gate_rows_grad = (hidden_grad * up_value * sigma * (1.0 + gate_value * (1.0 - sigma))).astype(
        jnp.bfloat16
    )
    acts = jnp.concatenate([gate_rows_grad, up_rows_grad, hidden], axis=1)
    acts = gather(acts, GROUP, 8).reshape(8 * CAP, 3 * hid)
    row_grads, hidden = acts[:, : 2 * hid], acts[:, 2 * hid :]

    terms = jnp.concatenate(
        [contract(row_grads, rows, 0, 0), contract(hidden, carried, 0, 0)], axis=0
    ).astype(jnp.bfloat16)
    terms = terms.reshape(3 * hid, 4, feat).transpose(1, 0, 2)
    here = lax.axis_index("zh")
    parts = [lax.dynamic_index_in_dim(terms, (here + d) % 4, 0, False) for d in range(4)]
    moved = [shift(parts[d], d) for d in (1, 2, 3)]
    row_grad = contract(row_grads, gate_up, 1, 0).astype(jnp.bfloat16)
    row_grad = row_grad.reshape(4, 2, CAP, 4 * feat)
    row_grad = once(grad_chain, row_grad, (WINDOW, CAP, feat))
    summed = parts[0].astype(jnp.float32) + row_grad[0, :1, :1].astype(jnp.float32) * 0
    for part in moved:
        summed = summed + part.astype(jnp.float32)
    summed = summed.astype(jnp.bfloat16)
    gate_grad, up_grad = summed[:hid].T, summed[hid : 2 * hid].T
    down_grad = summed[2 * hid :]

    x_grad = contract(picker, row_grad.reshape(WINDOW * CAP, feat), 0, 0).astype(jnp.bfloat16)
    return (x_grad, gate_grad, up_grad, down_grad)


def solution(mesh):
    fine = Mesh(mesh.devices.reshape(SHAPE), AXES)
    placed = (
        P(FSDP, EXPERT),
        P(FSDP, EXPERT),
        P(FSDP, None),
        P(FSDP, None),
        P(FSDP, EXPERT),
        P(FSDP, EXPERT),
        P(EXPERT, FSDP),
    )
    return jax.shard_map(
        shards,
        mesh=fine,
        in_specs=placed,
        out_specs=(P(FSDP, EXPERT), P(FSDP, EXPERT), P(FSDP, EXPERT), P(EXPERT, FSDP)),
        check_vma=False,
    )
```

```python
import jax
import jax.numpy as jnp
from jax import lax
from jax.sharding import Mesh, PartitionSpec as P

CAP = 64
WINDOW = 4
SHAPE = (4, 2, 4, 4, 2, 2, 2)
AXES = ("zp", "l", "x", "zh", "y_high", "y_low", "c")
EXPERT = ("zp", "l", "x")
FSDP = ("zh", "y_high", "y_low", "c")
PIECE = ("x", "l")
GROUP = ("y_low", "c", "y_high")


def contract(left, right, left_dim, right_dim):
    return lax.dot_general(
        left, right, (((left_dim,), (right_dim,)), ((), ())), preferred_element_type=jnp.float32
    )


def gather(block, axis, size):
    copies = jnp.broadcast_to(block[None], (size,) + block.shape)
    return lax.all_to_all(copies, axis, 0, 0)


def exchange(blocks, axis):
    return lax.all_to_all(blocks, axis, 0, 0)


def swap(block, piece_flip=0, group_flip=0):
    pairs = [
        (piece * 8 + group, (group ^ piece_flip) * 8 + (piece ^ group_flip))
        for piece in range(8)
        for group in range(8)
    ]
    return lax.ppermute(block, ("l", "x", "y_high", "y_low", "c"), pairs)


def select(probs, ids):
    window = jnp.arange(WINDOW, dtype=jnp.int32)
    hit = ids[None] == window[:, None, None]
    weight = jnp.sum(jnp.where(hit, probs[None], 0.0), axis=2)
    chosen = jnp.any(hit, axis=2)
    count = ids.shape[0]
    before = jnp.arange(count)[:, None] <= jnp.arange(count)[None, :]
    place = jnp.dot(
        chosen.astype(jnp.bfloat16), before.astype(jnp.bfloat16), preferred_element_type=jnp.float32
    ).astype(jnp.int32)
    slots = jnp.arange(1, CAP + 1, dtype=jnp.int32)
    picker = chosen[:, None, :] & (place[:, None, :] == slots[None, :, None])
    row_weight = jnp.sum(jnp.where(picker, weight[:, None, :], 0.0), axis=2)
    return picker.reshape(WINDOW * CAP, count).astype(jnp.bfloat16), row_weight.reshape(-1)


def once(step, value, out_shape):
    turns = 1 + lax.axis_index("x") // 4
    start = (jnp.int32(0), value, jnp.zeros(out_shape, jnp.bfloat16))
    return lax.while_loop(
        lambda state: state[0] < turns,
        lambda state: (state[0] + 1, state[1], step(state[1] + state[0].astype(jnp.bfloat16))),
        start,
    )[2]


def ordered(same, other):
    low = lax.axis_index("l") == 0
    return jnp.where(low, same, other), jnp.where(low, other, same)


def token_chain(both, weights):
    both = exchange(both, "zp") + weights[:1, :1] * 0
    feat = both.shape[2] // 2
    both = both.reshape(4, CAP, 2, feat).transpose(1, 2, 0, 3).reshape(CAP, 8 * feat)
    both = jnp.stack(ordered(swap(both), swap(both, piece_flip=4)))
    return gather(both, "x", 4).reshape(8 * CAP, 8 * feat)


def piece_sum(row_grad):
    row_grad = jnp.sum(exchange(row_grad, "x").astype(jnp.float32), axis=0).astype(jnp.bfloat16)
    return jnp.stack(ordered(row_grad[0], row_grad[1]))


def grad_chain(row_grad):
    feat = row_grad.shape[2] // 4
    same, other = swap(row_grad[0]), swap(row_grad[1], group_flip=4)
    row_grad = (same.astype(jnp.float32) + other.astype(jnp.float32)).astype(jnp.bfloat16)
    return exchange(row_grad.reshape(CAP, 4, feat).transpose(1, 0, 2), "zp")


def shift(block, d):
    return lax.ppermute(block, "zh", [(j, (j + d) % 4) for j in range(4)])


def shards(tokens, out_grad, route_probs, expert_ids, gate_weight, up_weight, down_weight):
    hid, feat = down_weight.shape
    own = jnp.concatenate([gate_weight.T, up_weight.T, down_weight], axis=0)
    weights = lax.all_gather(own, "zh")
    weights = jnp.concatenate(list(weights), axis=1)
    gate_up, down = weights[: 2 * hid], weights[2 * hid :]

    picker, row_weight = select(route_probs, expert_ids)
    picked = jnp.dot(picker, tokens, preferred_element_type=jnp.float32).astype(jnp.bfloat16)
    cot_rows = jnp.dot(picker, out_grad, preferred_element_type=jnp.float32)
    carried = (row_weight[:, None] * cot_rows).astype(jnp.bfloat16)
    both = jnp.concatenate([picked, carried], axis=1).reshape(WINDOW, CAP, 2 * feat)
    both = token_chain(both, weights)
    rows, carried = both[:, : 4 * feat], both[:, 4 * feat :]

    parts = jnp.concatenate(
        [contract(rows, gate_up, 1, 1), contract(carried, down, 1, 1)], axis=1
    ).astype(jnp.bfloat16)
    values = jnp.sum(
        exchange(parts.reshape(8, CAP, 3 * hid), GROUP).astype(jnp.float32), axis=0
    )
    gate_value, up_value, hidden_grad = (
        values[:, :hid],
        values[:, hid : 2 * hid],
        values[:, 2 * hid :],
    )
    sigma = jax.nn.sigmoid(gate_value)
    active = gate_value * sigma
    hidden = (active * up_value).astype(jnp.bfloat16)
    up_rows_grad = (hidden_grad * active).astype(jnp.bfloat16)
    gate_rows_grad = (hidden_grad * up_value * sigma * (1.0 + gate_value * (1.0 - sigma))).astype(
        jnp.bfloat16
    )
    acts = jnp.concatenate([gate_rows_grad, up_rows_grad, hidden], axis=1)
    acts = gather(acts, GROUP, 8).reshape(8 * CAP, 3 * hid)
    row_grads, hidden = acts[:, : 2 * hid], acts[:, 2 * hid :]

    terms = jnp.concatenate(
        [contract(row_grads, rows, 0, 0), contract(hidden, carried, 0, 0)], axis=0
    ).astype(jnp.bfloat16)
    terms = terms.reshape(3 * hid, 4, feat).transpose(1, 0, 2)
    here = lax.axis_index("zh")
    parts = [lax.dynamic_index_in_dim(terms, (here + d) % 4, 0, False) for d in range(4)]
    half = 3 * hid // 2
    low, high = shift(parts[2][:half], 1), shift(parts[2][half:], 3)
    row_grad = contract(row_grads, gate_up, 1, 0).astype(jnp.bfloat16)
    row_grad = row_grad.reshape(4, 2, CAP, 4 * feat)
    row_grad = once(piece_sum, row_grad, (2, CAP, 4 * feat))
    after = row_grad[0, :1, :1] * 0
    ahead = parts[1] + jnp.concatenate([low, jnp.zeros_like(high)], axis=0) + after
    behind = parts[3] + jnp.concatenate([jnp.zeros_like(low), high], axis=0) + after
    row_grad = row_grad + (ahead[:1, :1] + behind[:1, :1]) * 0
    ahead, behind = shift(ahead, 1), shift(behind, 3)
    row_grad = once(grad_chain, row_grad, (WINDOW, CAP, feat))
    summed = parts[0].astype(jnp.float32) + row_grad[0, :1, :1].astype(jnp.float32) * 0
    summed = summed + ahead.astype(jnp.float32) + behind.astype(jnp.float32)
    summed = summed.astype(jnp.bfloat16)
    gate_grad, up_grad = summed[:hid].T, summed[hid : 2 * hid].T
    down_grad = summed[2 * hid :]

    x_grad = contract(picker, row_grad.reshape(WINDOW * CAP, feat), 0, 0).astype(jnp.bfloat16)
    return (x_grad, gate_grad, up_grad, down_grad)


def solution(mesh):
    fine = Mesh(mesh.devices.reshape(SHAPE), AXES)
    placed = (
        P(FSDP, EXPERT),
        P(FSDP, EXPERT),
        P(FSDP, None),
        P(FSDP, None),
        P(FSDP, EXPERT),
        P(FSDP, EXPERT),
        P(EXPERT, FSDP),
    )
    return jax.shard_map(
        shards,
        mesh=fine,
        in_specs=placed,
        out_specs=(P(FSDP, EXPERT), P(FSDP, EXPERT), P(FSDP, EXPERT), P(EXPERT, FSDP)),
        check_vma=False,
    )
```

```python
import jax
import jax.numpy as jnp
from jax import lax
from jax.sharding import Mesh, PartitionSpec as P

CAP = 64
WINDOW = 4
SHAPE = (4, 2, 4, 4, 2, 2, 2)
AXES = ("zp", "l", "x", "zh", "y_high", "y_low", "c")
EXPERT = ("zp", "l", "x")
FSDP = ("zh", "y_high", "y_low", "c")
PIECE = ("x", "l")
GROUP = ("y_low", "c", "y_high")


def contract(left, right, left_dim, right_dim):
    return lax.dot_general(
        left, right, (((left_dim,), (right_dim,)), ((), ())), preferred_element_type=jnp.float32
    )


def gather(block, axis, size):
    copies = jnp.broadcast_to(block[None], (size,) + block.shape)
    return lax.all_to_all(copies, axis, 0, 0)


def exchange(blocks, axis):
    return lax.all_to_all(blocks, axis, 0, 0)


def swap(block, piece_flip=0, group_flip=0):
    pairs = [
        (piece * 8 + group, (group ^ piece_flip) * 8 + (piece ^ group_flip))
        for piece in range(8)
        for group in range(8)
    ]
    return lax.ppermute(block, ("l", "x", "y_high", "y_low", "c"), pairs)


def select(probs, ids):
    window = jnp.arange(WINDOW, dtype=jnp.int32)
    hit = ids[None] == window[:, None, None]
    weight = jnp.sum(jnp.where(hit, probs[None], 0.0), axis=2)
    chosen = jnp.any(hit, axis=2)
    count = ids.shape[0]
    before = jnp.arange(count)[:, None] <= jnp.arange(count)[None, :]
    place = jnp.dot(
        chosen.astype(jnp.bfloat16), before.astype(jnp.bfloat16), preferred_element_type=jnp.float32
    ).astype(jnp.int32)
    slots = jnp.arange(1, CAP + 1, dtype=jnp.int32)
    picker = chosen[:, None, :] & (place[:, None, :] == slots[None, :, None])
    row_weight = jnp.sum(jnp.where(picker, weight[:, None, :], 0.0), axis=2)
    return picker.reshape(WINDOW * CAP, count).astype(jnp.bfloat16), row_weight.reshape(-1)


def once(step, value, out_shape):
    turns = 1 + lax.axis_index("x") // 4
    start = (jnp.int32(0), value, jnp.zeros(out_shape, jnp.bfloat16))
    return lax.while_loop(
        lambda state: state[0] < turns,
        lambda state: (state[0] + 1, state[1], step(state[1] + state[0].astype(jnp.bfloat16))),
        start,
    )[::2]


def ordered(same, other):
    low = lax.axis_index("l") == 0
    return jnp.where(low, same, other), jnp.where(low, other, same)


def token_chain(both):
    both = exchange(both, "zp")
    feat = both.shape[2] // 2
    both = both.reshape(4, CAP, 2, feat).transpose(1, 2, 0, 3).reshape(CAP, 8 * feat)
    both = jnp.stack(ordered(swap(both), swap(both, piece_flip=4)))
    return gather(both, "x", 4).reshape(8 * CAP, 8 * feat)


def grad_chain(row_grad):
    feat = row_grad.shape[3] // 4
    row_grad = jnp.sum(exchange(row_grad, "x").astype(jnp.float32), axis=0).astype(jnp.bfloat16)
    same, other = ordered(row_grad[0], row_grad[1])
    same, other = swap(same), swap(other, group_flip=4)
    row_grad = (same.astype(jnp.float32) + other.astype(jnp.float32)).astype(jnp.bfloat16)
    return exchange(row_grad.reshape(CAP, 4, feat).transpose(1, 0, 2), "zp")


def shards(tokens, out_grad, route_probs, expert_ids, gate_weight, up_weight, down_weight):
    hid, feat = down_weight.shape
    own = jnp.concatenate([gate_weight.T, up_weight.T, down_weight], axis=0)
    weights = lax.all_gather(own, ("c", "zh")).reshape(2, 4, 3 * hid, feat)

    picker, row_weight = select(route_probs, expert_ids)
    picked = jnp.dot(picker, tokens, preferred_element_type=jnp.float32).astype(jnp.bfloat16)
    cot_rows = jnp.dot(picker, out_grad, preferred_element_type=jnp.float32)
    carried = (row_weight[:, None] * cot_rows).astype(jnp.bfloat16)
    both = jnp.concatenate([picked, carried], axis=1).reshape(WINDOW, CAP, 2 * feat)
    turns, both = once(token_chain, both, (8 * CAP, 8 * feat))
    rows, carried = both[:, : 4 * feat], both[:, 4 * feat :]
    weights = lax.dynamic_index_in_dim(weights, lax.axis_index("c") + turns - 1, 0, False)
    weights = jnp.concatenate(list(weights), axis=1)
    gate_up, down = weights[: 2 * hid], weights[2 * hid :]

    parts = jnp.concatenate(
        [contract(rows, gate_up, 1, 1), contract(carried, down, 1, 1)], axis=1
    ).astype(jnp.bfloat16)
    values = jnp.sum(
        exchange(parts.reshape(8, CAP, 3 * hid), GROUP).astype(jnp.float32), axis=0
    )
    gate_value, up_value, hidden_grad = (
        values[:, :hid],
        values[:, hid : 2 * hid],
        values[:, 2 * hid :],
    )
    sigma = jax.nn.sigmoid(gate_value)
    active = gate_value * sigma
    hidden = (active * up_value).astype(jnp.bfloat16)
    up_rows_grad = (hidden_grad * active).astype(jnp.bfloat16)
    gate_rows_grad = (hidden_grad * up_value * sigma * (1.0 + gate_value * (1.0 - sigma))).astype(
        jnp.bfloat16
    )
    acts = jnp.concatenate([gate_rows_grad, up_rows_grad, hidden], axis=1)
    acts = gather(acts, GROUP, 8).reshape(8 * CAP, 3 * hid)
    row_grads, hidden = acts[:, : 2 * hid], acts[:, 2 * hid :]

    terms = jnp.concatenate(
        [contract(row_grads, rows, 0, 0), contract(hidden, carried, 0, 0)], axis=0
    ).astype(jnp.bfloat16)
    summed = lax.psum_scatter(terms.reshape(3 * hid, 4, feat).transpose(1, 0, 2), "zh")
    row_grad = contract(row_grads, gate_up, 1, 0).astype(jnp.bfloat16).reshape(4, 2, CAP, 4 * feat)
    turns, row_grad = once(grad_chain, row_grad, (WINDOW, CAP, feat))
    gate_grad, up_grad, down_grad = (
        jnp.where(turns > 0, summed[i * hid : (i + 1) * hid], 0) for i in range(3)
    )
    gate_grad, up_grad = gate_grad.T, up_grad.T

    x_grad = contract(picker, row_grad.reshape(WINDOW * CAP, feat), 0, 0).astype(jnp.bfloat16)
    return (x_grad, gate_grad, up_grad, down_grad)


def solution(mesh):
    fine = Mesh(mesh.devices.reshape(SHAPE), AXES)
    placed = (
        P(FSDP, EXPERT),
        P(FSDP, EXPERT),
        P(FSDP, None),
        P(FSDP, None),
        P(FSDP, EXPERT),
        P(FSDP, EXPERT),
        P(EXPERT, FSDP),
    )
    return jax.shard_map(
        shards,
        mesh=fine,
        in_specs=placed,
        out_specs=(P(FSDP, EXPERT), P(FSDP, EXPERT), P(FSDP, EXPERT), P(EXPERT, FSDP)),
        check_vma=False,
    )
```

```python
import jax
import jax.numpy as jnp
from jax import lax
from jax.sharding import Mesh, PartitionSpec as P

CAP = 64
WINDOW = 4
SHAPE = (4, 2, 4, 4, 4, 2)
AXES = ("zp", "l", "x", "zh", "y", "c")
EXPERT = ("zp", "l", "x")
FSDP = ("zh", "y", "c")
PIECE = ("l", "x")
GROUP = ("y", "c")


def contract(left, right, left_dim, right_dim):
    return lax.dot_general(
        left, right, (((left_dim,), (right_dim,)), ((), ())), preferred_element_type=jnp.float32
    )


def gather(block, axis, size):
    copies = jnp.broadcast_to(block[None], (size,) + block.shape)
    return lax.all_to_all(copies, axis, 0, 0)


def exchange(blocks, axis):
    return lax.all_to_all(blocks, axis, 0, 0)


def swap(block):
    pairs = [(piece * 8 + group, group * 8 + piece) for piece in range(8) for group in range(8)]
    return lax.ppermute(block, PIECE + GROUP, pairs)


def select(probs, ids):
    window = jnp.arange(WINDOW, dtype=jnp.int32)
    hit = ids[None] == window[:, None, None]
    weight = jnp.sum(jnp.where(hit, probs[None], 0.0), axis=2)
    chosen = jnp.any(hit, axis=2)
    count = ids.shape[0]
    before = jnp.arange(count)[:, None] <= jnp.arange(count)[None, :]
    place = jnp.dot(
        chosen.astype(jnp.bfloat16), before.astype(jnp.bfloat16), preferred_element_type=jnp.float32
    ).astype(jnp.int32)
    slots = jnp.arange(1, CAP + 1, dtype=jnp.int32)
    picker = chosen[:, None, :] & (place[:, None, :] == slots[None, :, None])
    row_weight = jnp.sum(jnp.where(picker, weight[:, None, :], 0.0), axis=2)
    return picker.reshape(WINDOW * CAP, count).astype(jnp.bfloat16), row_weight.reshape(-1)


def once(step, value, out_shape):
    turns = 1 + lax.axis_index("x") // 4
    start = (jnp.int32(0), value, jnp.zeros(out_shape, jnp.bfloat16))
    return lax.while_loop(
        lambda state: state[0] < turns,
        lambda state: (state[0] + 1, state[1], step(state[1] + state[0].astype(jnp.bfloat16))),
        start,
    )[::2]


def token_chain(both):
    both = exchange(both, "zp")
    feat = both.shape[2] // 2
    both = both.reshape(4, CAP, 2, feat).transpose(1, 2, 0, 3).reshape(CAP, 8 * feat)
    return gather(swap(both), PIECE, 8).reshape(8 * CAP, 8 * feat)


def grad_chain(row_grad):
    feat = row_grad.shape[2] // 4
    row_grad = exchange(row_grad, PIECE).astype(jnp.float32)
    row_grad = swap(jnp.sum(row_grad, axis=0).astype(jnp.bfloat16))
    return exchange(row_grad.reshape(CAP, 4, feat).transpose(1, 0, 2), "zp")


def shards(tokens, out_grad, route_probs, expert_ids, gate_weight, up_weight, down_weight):
    hid, feat = down_weight.shape
    own = jnp.concatenate([gate_weight.T, up_weight.T, down_weight], axis=0)
    weights = lax.all_gather(own, ("c", "zh")).reshape(2, 4, 3 * hid, feat)

    picker, row_weight = select(route_probs, expert_ids)
    picked = jnp.dot(picker, tokens, preferred_element_type=jnp.float32).astype(jnp.bfloat16)
    cot_rows = jnp.dot(picker, out_grad, preferred_element_type=jnp.float32)
    carried = (row_weight[:, None] * cot_rows).astype(jnp.bfloat16)
    both = jnp.concatenate([picked, carried], axis=1).reshape(WINDOW, CAP, 2 * feat)
    turns, both = once(token_chain, both, (8 * CAP, 8 * feat))
    rows, carried = both[:, : 4 * feat], both[:, 4 * feat :]
    weights = lax.dynamic_index_in_dim(weights, lax.axis_index("c") + turns - 1, 0, False)
    weights = jnp.concatenate(list(weights), axis=1)
    gate_up, down = weights[: 2 * hid], weights[2 * hid :]

    parts = jnp.concatenate(
        [contract(rows, gate_up, 1, 1), contract(carried, down, 1, 1)], axis=1
    ).astype(jnp.bfloat16)
    values = jnp.sum(
        exchange(parts.reshape(8, CAP, 3 * hid), GROUP).astype(jnp.float32), axis=0
    )
    gate_value, up_value, hidden_grad = (
        values[:, :hid],
        values[:, hid : 2 * hid],
        values[:, 2 * hid :],
    )
    sigma = jax.nn.sigmoid(gate_value)
    active = gate_value * sigma
    hidden = (active * up_value).astype(jnp.bfloat16)
    up_rows_grad = (hidden_grad * active).astype(jnp.bfloat16)
    gate_rows_grad = (hidden_grad * up_value * sigma * (1.0 + gate_value * (1.0 - sigma))).astype(
        jnp.bfloat16
    )
    acts = jnp.concatenate([gate_rows_grad, up_rows_grad, hidden], axis=1)
    acts = gather(acts, GROUP, 8).reshape(8 * CAP, 3 * hid)
    row_grads, hidden = acts[:, : 2 * hid], acts[:, 2 * hid :]

    terms = jnp.concatenate(
        [contract(row_grads, rows, 0, 0), contract(hidden, carried, 0, 0)], axis=0
    ).astype(jnp.bfloat16)
    summed = lax.psum_scatter(terms.reshape(3 * hid, 4, feat).transpose(1, 0, 2), "zh")
    row_grad = contract(row_grads, gate_up, 1, 0).astype(jnp.bfloat16).reshape(8, CAP, 4 * feat)
    turns, row_grad = once(grad_chain, row_grad, (WINDOW, CAP, feat))
    gate_grad, up_grad, down_grad = (
        jnp.where(turns > 0, summed[i * hid : (i + 1) * hid], 0) for i in range(3)
    )
    gate_grad, up_grad = gate_grad.T, up_grad.T

    x_grad = contract(picker, row_grad.reshape(WINDOW * CAP, feat), 0, 0).astype(jnp.bfloat16)
    return (x_grad, gate_grad, up_grad, down_grad)


def solution(mesh):
    fine = Mesh(mesh.devices.reshape(SHAPE), AXES)
    placed = (
        P(FSDP, EXPERT),
        P(FSDP, EXPERT),
        P(FSDP, None),
        P(FSDP, None),
        P(FSDP, EXPERT),
        P(FSDP, EXPERT),
        P(EXPERT, FSDP),
    )
    return jax.shard_map(
        shards,
        mesh=fine,
        in_specs=placed,
        out_specs=(P(FSDP, EXPERT), P(FSDP, EXPERT), P(FSDP, EXPERT), P(EXPERT, FSDP)),
        check_vma=False,
    )
```

```python
import jax
import jax.numpy as jnp
from jax import lax
from jax.sharding import Mesh, PartitionSpec as P

CAP = 64
WINDOW = 4
SHAPE = (4, 2, 4, 4, 4, 2)
AXES = ("zp", "l", "x", "zh", "y", "c")
EXPERT = ("zp", "l", "x")
FSDP = ("zh", "y", "c")
PIECE = ("l", "x")
GROUP = "y"


def contract(left, right, left_dim, right_dim):
    return lax.dot_general(
        left, right, (((left_dim,), (right_dim,)), ((), ())), preferred_element_type=jnp.float32
    )


def gather(block, axis, size):
    copies = jnp.broadcast_to(block[None], (size,) + block.shape)
    return lax.all_to_all(copies, axis, 0, 0)


def exchange(blocks, axis):
    return lax.all_to_all(blocks, axis, 0, 0)


def swap(block):
    pairs = [
        ((high * 2 + low) * 4 + group, (group * 2 + low) * 4 + high)
        for high in range(4)
        for low in range(2)
        for group in range(4)
    ]
    return lax.ppermute(block, PIECE + (GROUP,), pairs)


def select(probs, ids):
    window = jnp.arange(WINDOW, dtype=jnp.int32)
    hit = ids[None] == window[:, None, None]
    weight = jnp.sum(jnp.where(hit, probs[None], 0.0), axis=2)
    chosen = jnp.any(hit, axis=2)
    count = ids.shape[0]
    before = jnp.arange(count)[:, None] <= jnp.arange(count)[None, :]
    place = jnp.dot(
        chosen.astype(jnp.bfloat16), before.astype(jnp.bfloat16), preferred_element_type=jnp.float32
    ).astype(jnp.int32)
    slots = jnp.arange(1, CAP + 1, dtype=jnp.int32)
    picker = chosen[:, None, :] & (place[:, None, :] == slots[None, :, None])
    row_weight = jnp.sum(jnp.where(picker, weight[:, None, :], 0.0), axis=2)
    return picker.reshape(WINDOW * CAP, count).astype(jnp.bfloat16), row_weight.reshape(-1)


def once(step, value, out_shape):
    turns = 1 + lax.axis_index("x") // 4
    start = (jnp.int32(0), value, jnp.zeros(out_shape, jnp.bfloat16))
    return lax.while_loop(
        lambda state: state[0] < turns,
        lambda state: (state[0] + 1, state[1], step(state[1] + state[0].astype(jnp.bfloat16))),
        start,
    )[::2]


def token_chain(both):
    both = exchange(both, "zp")
    feat = both.shape[2] // 2
    both = both.reshape(4, CAP, 2, feat).transpose(1, 2, 0, 3).reshape(CAP, 8 * feat)
    return gather(swap(both), PIECE, 8)


def grad_chain(row_grad):
    feat = row_grad.shape[2] // 4
    row_grad = exchange(row_grad, PIECE).astype(jnp.float32)
    row_grad = swap(jnp.sum(row_grad, axis=0).astype(jnp.bfloat16))
    return exchange(row_grad.reshape(CAP, 4, feat).transpose(1, 0, 2), "zp")


def shards(tokens, out_grad, route_probs, expert_ids, gate_weight, up_weight, down_weight):
    hid, feat = down_weight.shape
    own = jnp.concatenate([gate_weight.T, up_weight.T, down_weight], axis=0)
    weights = lax.all_gather(own, ("c", "zh"))

    picker, row_weight = select(route_probs, expert_ids)
    picked = jnp.dot(picker, tokens, preferred_element_type=jnp.float32).astype(jnp.bfloat16)
    cot_rows = jnp.dot(picker, out_grad, preferred_element_type=jnp.float32)
    carried = (row_weight[:, None] * cot_rows).astype(jnp.bfloat16)
    both = jnp.concatenate([picked, carried], axis=1).reshape(WINDOW, CAP, 2 * feat)
    turns, both = once(token_chain, both, (8, CAP, 8 * feat))
    both = both.reshape(4, 2, CAP, 2, 4 * feat).transpose(3, 0, 2, 1, 4)
    rows, carried = both.reshape(2, 4 * CAP, 8 * feat)
    weights = jnp.where(turns > 0, weights, 0).transpose(1, 0, 2).reshape(3 * hid, 8 * feat)
    gate_up, down = weights[: 2 * hid], weights[2 * hid :]

    parts = jnp.concatenate(
        [contract(rows, gate_up, 1, 1), contract(carried, down, 1, 1)], axis=1
    ).astype(jnp.bfloat16)
    values = jnp.sum(
        exchange(parts.reshape(4, CAP, 3 * hid), GROUP).astype(jnp.float32), axis=0
    )
    gate_value, up_value, hidden_grad = (
        values[:, :hid],
        values[:, hid : 2 * hid],
        values[:, 2 * hid :],
    )
    sigma = jax.nn.sigmoid(gate_value)
    active = gate_value * sigma
    hidden = (active * up_value).astype(jnp.bfloat16)
    up_rows_grad = (hidden_grad * active).astype(jnp.bfloat16)
    gate_rows_grad = (hidden_grad * up_value * sigma * (1.0 + gate_value * (1.0 - sigma))).astype(
        jnp.bfloat16
    )
    acts = jnp.concatenate([gate_rows_grad, up_rows_grad, hidden], axis=1)
    acts = gather(acts, GROUP, 4).reshape(4 * CAP, 3 * hid)
    row_grads, hidden = acts[:, : 2 * hid], acts[:, 2 * hid :]

    terms = jnp.concatenate(
        [contract(row_grads, rows, 0, 0), contract(hidden, carried, 0, 0)], axis=0
    ).astype(jnp.bfloat16)
    terms = exchange(terms.reshape(3 * hid, 2, 4, feat).transpose(1, 2, 0, 3), "c")
    terms = jnp.sum(terms.astype(jnp.float32), axis=0).astype(jnp.bfloat16)
    summed = lax.psum_scatter(terms, "zh")
    row_grad = contract(row_grads, gate_up, 1, 0).astype(jnp.bfloat16)
    row_grad = row_grad.reshape(4, CAP, 2, 4 * feat).transpose(0, 2, 1, 3)
    row_grad = row_grad.reshape(8, CAP, 4 * feat)
    turns, row_grad = once(grad_chain, row_grad, (WINDOW, CAP, feat))
    gate_grad, up_grad, down_grad = (
        jnp.where(turns > 0, summed[i * hid : (i + 1) * hid], 0) for i in range(3)
    )
    gate_grad, up_grad = gate_grad.T, up_grad.T

    x_grad = contract(picker, row_grad.reshape(WINDOW * CAP, feat), 0, 0).astype(jnp.bfloat16)
    return (x_grad, gate_grad, up_grad, down_grad)


def solution(mesh):
    fine = Mesh(mesh.devices.reshape(SHAPE), AXES)
    placed = (
        P(FSDP, EXPERT),
        P(FSDP, EXPERT),
        P(FSDP, None),
        P(FSDP, None),
        P(FSDP, EXPERT),
        P(FSDP, EXPERT),
        P(EXPERT, FSDP),
    )
    return jax.shard_map(
        shards,
        mesh=fine,
        in_specs=placed,
        out_specs=(P(FSDP, EXPERT), P(FSDP, EXPERT), P(FSDP, EXPERT), P(EXPERT, FSDP)),
        check_vma=False,
    )
```
